512 devices in a mesh: batch: 8 (over y, core), seq: 64 (over z, x).
Axes of the slice: x: 4, y: 4, z: 16, core: 2. Of those that a mesh axis runs over, the one named last changes fastest.
Arguments:
- queries: bfloat16 [131072, 1024], P(('batch', 'seq')), parts along dimension 0, may hold values from -12 to 12
- keys_values: bfloat16 [2, 131072, 1024], P(None, ('batch', 'seq')), parts along dimension 1, may hold values from -6 to 6
- random_blocks: int32 [2048, 16, 3], P(('batch', 'seq')), parts along dimension 0, may hold values from 0 to 255, as said below
- global_blocks: int32 [16], P('batch'), parts along dimension 0, may hold values from 0 to 255, as said below
- out_proj: bfloat16 [1024, 1024], P('seq'), may hold values from -0.375 to 0.375
Outputs:
- attended: bfloat16 [131072, 1024], P(('batch', 'seq')), parts along dimension 0
The draws below stay inside these ranges and needn't reach their ends.
There are 8 independent parts, one for each index of `batch`. The reference program is written for one: setup_inputs(seed, part) draws one part's arguments, and reference() takes and returns one part's arrays. A program takes and returns all parts, laid end to end along the dimension named above; an argument that names none is the same for every part. Nothing has to cross between parts.
Inputs may be any that keep to these rules, and one draw needn't show every extreme that they name: Each list random_blocks[i, h] names 3 different blocks. Device d holds blocks d * 4 to (d + 1) * 4 - 1. Among the 64 lists of one device's query blocks no block is named more than 2 times and some block exactly 2 times; the blocks of any one device are named at most 6 times in all and those of some device exactly 6 times. The 2 global blocks are different; the last of them, global_blocks[1], is the sequence's last block 255.
All inputs are finite; a program needn't handle non-finite values.
Results may differ from the reference program's by a relative error of at most 0.0052.
Values may be sent and summed in bfloat16 or wider, within the bound.
A program may use at most 192 MiB of HBM per device.

```python
import jax
import jax.numpy as jnp
from jax import lax

D = 1024
H = 16
BLK = 64
R = 3
G = 2
QB_DEV = 4
DH = 64
NB = 256
SEQ = 16384
HOT = 32


def global_pick(key):
    others = jax.random.permutation(jax.random.fold_in(key, 17), NB - 1)[:G - 1].astype(jnp.int32)
    return jnp.concatenate([others, jnp.array([NB - 1], jnp.int32)])


def drawn_fields(key):
    base = jax.random.fold_in(key, 29)
    streams = jax.random.split(base, 3)
    queries = 3.0 * jax.random.truncated_normal(streams[0], -4.0, 4.0, (SEQ, D), jnp.float32)
    keys = jax.random.truncated_normal(streams[1], -4.0, 4.0, (SEQ, D), jnp.float32)
    values = jax.random.truncated_normal(streams[2], -4.0, 4.0, (SEQ, D), jnp.float32)
    return (queries, jnp.stack([keys, values]))


def draw_queries(key, part):
    return drawn_fields(key)[0].astype(jnp.bfloat16)


def draw_keys_values(key, part):
    return drawn_fields(key)[1].astype(jnp.bfloat16)


def draw_global_blocks(key, part):
    return global_pick(key)


def draw_random_blocks(key, part):
    owners_total = NB // QB_DEV
    entries = QB_DEV * H * R
    streams = jax.random.split(jax.random.fold_in(key, 41), 2)
    window_start = jax.random.randint(streams[0], (owners_total, 1), 0, owners_total)
    rotation = jax.random.randint(streams[1], (owners_total, owners_total), 0, QB_DEV)
    entry = jnp.arange(entries, dtype=jnp.int32)[None, :]
    owner = (window_start + entry % HOT) % owners_total
    rank = entry // HOT
    device = jnp.broadcast_to(jnp.arange(owners_total, dtype=jnp.int32)[:, None], owner.shape)
    local = (rank + rotation[device, owner]) % QB_DEV
    chosen = owner * QB_DEV + local
    return chosen.reshape(NB, H, R).astype(jnp.int32)


def level_of(stream_key, dims, cuts, low, largest):
    level, own = 1.0, jax.random.fold_in(stream_key, 6)
    for dim, shards_of in cuts:
        heights = jnp.exp(jax.random.uniform(jax.random.fold_in(own, dim), (shards_of,), jnp.float32, low / len(cuts), largest / len(cuts)))
        level = level * jnp.repeat(heights, dims[dim] // shards_of).reshape([-1 if axis == dim else 1 for axis in range(len(dims))])
    return level


def bell_draw(rng, dims, deviation, reach, cuts=(), kind=jnp.bfloat16):
    loudness = level_of(rng, dims, cuts, -0.22, 0.18) if cuts else 1.0
    result = jax.random.normal(rng, dims, jnp.float32) * deviation * loudness
    return jnp.minimum(jnp.maximum(result, -reach), reach).astype(kind)


def setup_inputs(seed: int = 0, part: int = 0) -> dict:
    arg_keys = jax.random.split(jax.random.key(seed), 6)
    part_splits = jax.random.split(jax.random.fold_in(arg_keys[5], part), 6)
    queries = draw_queries(jax.random.fold_in(jax.random.fold_in(arg_keys[5], part), 71), part)
    keys_values = draw_keys_values(jax.random.fold_in(jax.random.fold_in(arg_keys[5], part), 71), part)
    random_blocks = draw_random_blocks(jax.random.fold_in(jax.random.fold_in(arg_keys[5], part), 71), part)
    global_blocks = draw_global_blocks(jax.random.fold_in(jax.random.fold_in(arg_keys[5], part), 71), part)
    out_proj = bell_draw(arg_keys[4], (D, D), (D // 4) ** -0.5, 0.375, ((0, 64),))
    return {"queries": queries, "keys_values": keys_values, "random_blocks": random_blocks, "global_blocks": global_blocks, "out_proj": out_proj}


masked_score = -1e30


def reference(queries, keys_values, random_blocks, global_blocks, out_proj):
    block_total = SEQ // BLK
    score_scale = DH ** -0.5
    query_blocks = queries.reshape(block_total, BLK, H, DH)
    key_blocks = keys_values[0].reshape(block_total, BLK, H, DH)
    value_blocks = keys_values[1].reshape(block_total, BLK, H, DH)
    key_heads = key_blocks.transpose(0, 2, 1, 3)
    value_heads = value_blocks.transpose(0, 2, 1, 3)
    glob_keys = key_blocks[global_blocks].reshape(G * BLK, H, DH).astype(jnp.float32)
    glob_vals = value_blocks[global_blocks].reshape(G * BLK, H, DH).astype(jnp.float32)
    head_range = jnp.arange(H, dtype=jnp.int32)

    def attend(block_index):
        qblock = query_blocks[block_index].astype(jnp.float32)
        neighbours = block_index + jnp.arange(-1, 2, dtype=jnp.int32)
        inside = (neighbours >= 0) & (neighbours < block_total)
        clipped = jnp.clip(neighbours, 0, block_total - 1)
        win_keys = key_blocks[clipped].reshape(3 * BLK, H, DH).astype(jnp.float32)
        win_vals = value_blocks[clipped].reshape(3 * BLK, H, DH).astype(jnp.float32)
        chosen = random_blocks[block_index]
        rand_keys = key_heads[chosen, head_range[:, None]].reshape(H, R * BLK, DH).astype(jnp.float32)
        rand_vals = value_heads[chosen, head_range[:, None]].reshape(H, R * BLK, DH).astype(jnp.float32)
        win_scores = jnp.einsum("qhd,khd->hqk", qblock, win_keys)
        glob_scores = jnp.einsum("qhd,khd->hqk", qblock, glob_keys)
        rand_scores = jnp.einsum("qhd,hkd->hqk", qblock, rand_keys)
        scores = jnp.concatenate([win_scores, glob_scores, rand_scores], axis=2) * score_scale
        keep_mask = jnp.concatenate([jnp.repeat(inside, BLK), jnp.ones((G * BLK + R * BLK,), bool)])
        scores = jnp.where(keep_mask[None, None, :], scores, masked_score)
        row_max = jnp.max(scores, axis=2)
        weights = jnp.exp(scores - row_max[:, :, None])
        totals = jnp.sum(weights, axis=2)
        rounded = weights.astype(jnp.bfloat16).astype(jnp.float32)
        mixed = jnp.einsum("hqk,khd->qhd", rounded[:, :, :3 * BLK], win_vals)
        mixed = mixed + jnp.einsum("hqk,khd->qhd", rounded[:, :, 3 * BLK:3 * BLK + G * BLK], glob_vals)
        mixed = mixed + jnp.einsum("hqk,hkd->qhd", rounded[:, :, 3 * BLK + G * BLK:], rand_vals)
        return (mixed / totals.T[:, :, None]).astype(jnp.bfloat16).reshape(BLK, H * DH)

    context = lax.map(attend, jnp.arange(block_total, dtype=jnp.int32))
    glob_query = queries.reshape(block_total, BLK, H * DH)[global_blocks].reshape(G * BLK, H * DH)
    all_keys = keys_values[0]
    all_vals = keys_values[1]

    def glob_head(head):
        start_col = (head * DH).astype(jnp.int32)
        query_head = lax.dynamic_slice_in_dim(glob_query, start_col, DH, 1).astype(jnp.float32)
        key_head = lax.dynamic_slice_in_dim(all_keys, start_col, DH, 1).astype(jnp.float32)
        value_head = lax.dynamic_slice_in_dim(all_vals, start_col, DH, 1).astype(jnp.float32)
        scores = jnp.dot(query_head, key_head.T, precision=lax.Precision.HIGHEST) * score_scale
        weights = jnp.exp(scores - jnp.max(scores, axis=1)[:, None])
        sums = jnp.sum(weights, axis=1)
        weighted = jnp.dot(weights, value_head, precision=lax.Precision.HIGHEST)
        return weighted / sums[:, None]

    per_head = lax.map(glob_head, jnp.arange(H, dtype=jnp.int32))
    glob_ctx = per_head.transpose(1, 0, 2).reshape(G, BLK, H * DH).astype(jnp.bfloat16)
    context = context.at[global_blocks].set(glob_ctx)
    flat_context = context.reshape(SEQ, H * DH)
    return jnp.dot(flat_context, out_proj, preferred_element_type=jnp.float32).astype(jnp.bfloat16)
```

```python
import functools

import jax
import jax.numpy as jnp
from jax import lax
from jax.experimental import pallas as pl
from jax.experimental.pallas import tpu as pltpu
from jax.sharding import PartitionSpec as P

H = 16
BLK = 64
R = 3
X = 4
G = 2
HALF = 64
LANES = 128
MESH = pl.DeviceIdType.MESH
NEG = -1e30
F32 = jnp.float32
BF16 = jnp.bfloat16


def swap(x):
    return pltpu.roll(x.astype(F32), HALF, 1).astype(x.dtype)


def dot_nt(a, b):
    return lax.dot_general(a, b, (((1,), (1,)), ((), ())), preferred_element_type=F32)


def dot_nn(a, b):
    return lax.dot_general(a, b, (((1,), (0,)), ((), ())), preferred_element_type=F32)


def kernel(
    nz, bd, scale2,
    gb_ref, q_ref, kv_ref, rb_ref, ctx_ref,
    qpack, kvpack, kvf, q_in, rb_in, rb_s, qc_in, gpart, gout, gkv, o_pack, o_in, stat,
    q_send, q_recv, rb_send, rb_recv, kv_send, kv_recv, o_send, o_recv,
    r_send, l_send, fl_recv, fr_recv, ha_send, hb_send, oa_recv, ob_recv,
    qc_send, qc_recv, gp_send, gp_recv, rbs_sem,
):
    tok = bd * BLK
    half_tok = tok // 2
    half_bd = bd // 2
    nb = nz * X * bd
    batch = lax.axis_index("batch")
    me = lax.axis_index("seq")
    z = me // X
    x = lax.rem(me, X)
    right = lax.rem(x + 1, X)
    left = lax.rem(x + X - 1, X)

    def dev(zz, xx):
        return (batch, zz * X + xx)

    def remote(src, dst, send, recv, where):
        return pltpu.make_async_remote_copy(
            src_ref=src, dst_ref=dst, send_sem=send, recv_sem=recv, device_id=where, device_id_type=MESH
        )

    def order(i):
        return lax.rem(jnp.where(lax.rem(i, 2) == 1, (i + 1) // 2, nz - i // 2), nz)

    def dest_of(i):
        return lax.rem(z + order(i), nz)

    def src_of(i):
        return lax.rem(z + nz - order(i), nz)

    def rows(zz, xx, first=0, count=None):
        return pl.ds(1 + (zz * X + xx) * bd + first, bd if count is None else count)

    barrier = pltpu.get_barrier_semaphore()

    @pl.loop(1, nz)
    def _(i):
        pl.semaphore_signal(barrier, inc=1, device_id=dev(lax.rem(z + i, nz), x), device_id_type=MESH)

    for d in range(1, X):
        pl.semaphore_signal(barrier, inc=1, device_id=dev(z, lax.rem(x + d, X)), device_id_type=MESH)

    lo_q = lax.broadcasted_iota(jnp.int32, (half_tok, LANES), 1) < HALF
    for p in range(nz // 2):
        cols = slice(p * LANES, (p + 1) * LANES)
        top, bot = q_ref[:half_tok, cols], q_ref[half_tok:, cols]
        qpack[2 * p] = jnp.where(lo_q, top, swap(bot)).reshape(half_bd, BLK, LANES)
        qpack[2 * p + 1] = jnp.where(lo_q, swap(top), bot).reshape(half_bd, BLK, LANES)

    pl.semaphore_wait(barrier, nz - 1 + X - 1)

    def q_copy(dz):
        return remote(qpack.at[dz], q_in.at[z], q_send.at[dz], q_recv.at[z], dev(dz, x))

    def rb_copy(dz):
        return remote(rb_ref.at[dz], rb_in.at[z], rb_send.at[dz], rb_recv.at[z], dev(dz, x))

    def kv_copy(dz):
        return remote(kvpack.at[dz], kvf.at[rows(z, x)], kv_send.at[dz], kv_recv.at[z], dev(dz, x))

    def o_copy(dz):
        return remote(o_pack.at[dz], o_in.at[z], o_send.at[dz], o_recv.at[z], dev(dz, x))

    @pl.loop(1, nz)
    def _(i):
        dz = dest_of(i)
        q_copy(dz).start()
        rb_copy(dz).start()

    lo_t = lax.broadcasted_iota(jnp.int32, (tok, LANES), 1) < HALF
    for p in range(nz // 2):
        cols = slice(p * LANES, (p + 1) * LANES)
        keys, vals = kv_ref[0, :, cols], kv_ref[1, :, cols]
        kvpack[2 * p] = jnp.where(lo_t, keys, swap(vals)).reshape(bd, BLK, LANES)
        kvpack[2 * p + 1] = jnp.where(lo_t, swap(keys), vals).reshape(bd, BLK, LANES)

    @pl.loop(1, nz)
    def _(i):
        kv_copy(dest_of(i)).start()

    q_in[z] = qpack[z]
    rb_in[z] = rb_ref[z]
    kvf[rows(z, x)] = kvpack[z]
    kvf[0] = jnp.zeros((BLK, LANES), BF16)
    kvf[nb + 1] = jnp.zeros((BLK, LANES), BF16)

    @pl.loop(1, nz)
    def _(i):
        zs = src_of(i)
        remote(qpack.at[zs], q_in.at[zs], q_send.at[zs], q_recv.at[zs], dev(zs, x)).wait_recv()
        remote(rb_ref.at[zs], rb_in.at[zs], rb_send.at[zs], rb_recv.at[zs], dev(zs, x)).wait_recv()

    to_smem = pltpu.make_async_copy(rb_in, rb_s, rbs_sem)
    to_smem.start()

    lo_b = lax.broadcasted_iota(jnp.int32, (BLK, LANES), 1) < HALF

    def spread(number):
        return jnp.broadcast_to(number, (BLK, LANES))

    for g in range(G):
        block = gb_ref[g]
        within = lax.rem(block, bd)
        tile = q_in[lax.div(block, bd * X), lax.rem(within, half_bd)]
        tile = jnp.where(spread(within) >= half_bd, swap(tile), tile)
        qc_in[x, g] = jnp.where(lo_b, tile, jnp.zeros_like(tile))

    def qc_copy(d):
        return remote(qc_in.at[x], qc_in.at[x], qc_send.at[d], qc_recv.at[x], dev(z, lax.rem(x + d, X)))

    def qc_wait(d):
        xs = lax.rem(x + d, X)
        remote(qc_in.at[xs], qc_in.at[xs], qc_send.at[d], qc_recv.at[xs], dev(z, xs)).wait_recv()

    for d in range(1, X):
        qc_copy(d).start()
    for d in range(1, X):
        qc_wait(d)

    glob_q = jnp.concatenate(
        [qc_in[lax.rem(lax.div(gb_ref[g], bd), X), g] for g in range(G)], axis=0
    )
    gout[...] = jnp.zeros_like(gout)
    stat[0] = jnp.full((G * BLK, LANES), NEG, F32)
    stat[1] = jnp.zeros((G * BLK, LANES), F32)

    def right_copy(zs):
        part = kvf.at[rows(zs, x)]
        return remote(part, part, r_send.at[zs], fl_recv.at[zs], dev(z, right))

    def left_copy(zs):
        part = kvf.at[rows(zs, x)]
        return remote(part, part, l_send.at[zs], fr_recv.at[zs], dev(z, left))

    def from_left(zs):
        part = kvf.at[rows(zs, left)]
        return remote(part, part, r_send.at[zs], fl_recv.at[zs], dev(z, left))

    def from_right(zs):
        part = kvf.at[rows(zs, right)]
        return remote(part, part, l_send.at[zs], fr_recv.at[zs], dev(z, right))

    def half_right(zs):
        part = kvf.at[rows(zs, left, 0, half_bd)]
        return remote(part, part, ha_send.at[zs], oa_recv.at[zs], dev(z, right))

    def half_left(zs):
        part = kvf.at[rows(zs, right, half_bd, half_bd)]
        return remote(part, part, hb_send.at[zs], ob_recv.at[zs], dev(z, left))

    opposite = lax.rem(x + 2, X)

    def half_a(zs):
        part = kvf.at[rows(zs, opposite, 0, half_bd)]
        return remote(part, part, ha_send.at[zs], oa_recv.at[zs], dev(z, left))

    def half_b(zs):
        part = kvf.at[rows(zs, opposite, half_bd, half_bd)]
        return remote(part, part, hb_send.at[zs], ob_recv.at[zs], dev(z, right))

    def pass_on(zs):
        from_left(zs).wait_recv()
        half_right(zs).start()
        from_right(zs).wait_recv()
        half_left(zs).start()

    @pl.loop(0, nz)
    def _(i):
        zs = src_of(i)

        @pl.when(i > 0)
        def _():
            part = kvf.at[rows(zs, x)]
            remote(part, part, kv_send.at[zs], kv_recv.at[zs], dev(zs, x)).wait_recv()

        right_copy(zs).start()
        left_copy(zs).start()
        chunk = kvf[rows(zs, x)].reshape(tok, LANES)
        scores = dot_nt(glob_q, chunk)
        old_max = stat[0]
        new_max = jnp.maximum(old_max, jnp.max(scores, axis=1, keepdims=True))
        shrink = jnp.exp2((old_max - new_max) * scale2)
        weights = jnp.exp2((scores - new_max[:, :1]) * scale2)
        stat[0] = new_max
        stat[1] = stat[1] * shrink + jnp.sum(weights, axis=1, keepdims=True)
        gout[...] = gout[...] * shrink + dot_nn(weights.astype(BF16), chunk)

        @pl.when(i > 0)
        def _():
            pass_on(src_of(i - 1))

    pass_on(src_of(nz - 1))

    lane_g = lax.broadcasted_iota(jnp.int32, (G * BLK, LANES), 1)
    gpart[x] = jnp.where(lane_g < HALF // 2, stat[0], jnp.where(lane_g < HALF, stat[1], gout[...]))

    def gp_copy(d):
        return remote(gpart.at[x], gpart.at[x], gp_send.at[d], gp_recv.at[x], dev(z, lax.rem(x + d, X)))

    def gp_wait(d):
        xs = lax.rem(x + d, X)
        remote(gpart.at[xs], gpart.at[xs], gp_send.at[d], gp_recv.at[xs], dev(z, xs)).wait_recv()

    for d in range(1, X):
        gp_copy(d).start()

    @pl.loop(0, nz)
    def _(i):
        zs = src_of(i)
        half_a(zs).wait_recv()
        half_b(zs).wait_recv()

    for d in range(1, X):
        gp_wait(d)
    top_max = functools.reduce(jnp.maximum, [gpart[c][:, :1] for c in range(X)])
    glob_total = jnp.zeros((G * BLK, 1), F32)
    glob_acc = jnp.zeros((G * BLK, LANES), F32)
    for c in range(X):
        part = gpart[c]
        factor = jnp.exp2((part[:, :1] - top_max) * scale2)
        glob_total = glob_total + part[:, HALF // 2:HALF // 2 + 1] * factor
        glob_acc = glob_acc + part * factor
    gout[...] = glob_acc / glob_total

    for g in range(G):
        gkv[g * BLK:(g + 1) * BLK, :] = kvf[1 + gb_ref[g]]
    to_smem.wait()

    key_lane = lax.broadcasted_iota(jnp.int32, (BLK, (3 + R + G) * BLK), 1)

    @pl.loop(0, nz)
    def _(i):
        zs = src_of(i)
        packed = q_in[zs].reshape(half_tok, LANES)
        zero = jnp.zeros_like(packed)
        halves = (jnp.where(lo_q, packed, zero), jnp.where(lo_q, swap(packed), zero))
        outs = []
        for j in range(bd):
            block = (zs * X + x) * bd + j
            first = (j % half_bd) * BLK
            qb = halves[j // half_bd][first:first + BLK, :]
            parts = [kvf[block + w] for w in range(3)]
            for r in range(R):
                pick = rb_s[zs, 0, j * R + r]
                parts.append(kvf[1 + pick])
            parts.append(gkv[...])
            keyval = jnp.concatenate(parts, axis=0)
            scores = dot_nt(qb, keyval)
            if j == 0:
                scores = jnp.where((key_lane < BLK) & (block == 0), NEG, scores)
            if j == bd - 1:
                outside = (key_lane >= 2 * BLK) & (key_lane < 3 * BLK) & (block == nb - 1)
                scores = jnp.where(outside, NEG, scores)
            row_max = jnp.max(scores, axis=1, keepdims=True)
            weights = jnp.exp2((scores - row_max) * scale2)
            total = jnp.sum(weights, axis=1, keepdims=True)
            mixed = dot_nn(weights.astype(BF16), keyval) / total
            for g in range(G):
                mixed = jnp.where(spread(gb_ref[g]) == block, gout[g * BLK:(g + 1) * BLK, :], mixed)
            outs.append(mixed)
        low = jnp.concatenate(outs[:half_bd], axis=0)
        high = jnp.concatenate(outs[half_bd:], axis=0)
        o_pack[zs] = jnp.where(lo_q, pltpu.roll(low, HALF, 1), high).astype(BF16)

        @pl.when(i > 0)
        def _():
            o_copy(zs).start()

    o_in[z] = o_pack[z]

    @pl.loop(1, nz)
    def _(i):
        zs = src_of(i)
        remote(o_pack.at[zs], o_in.at[zs], o_send.at[zs], o_recv.at[zs], dev(zs, x)).wait_recv()

    for p in range(nz // 2):
        cols = slice(p * LANES, (p + 1) * LANES)
        even, odd = o_in[2 * p], o_in[2 * p + 1]
        ctx_ref[:half_tok, cols] = jnp.where(lo_q, even, swap(odd))
        ctx_ref[half_tok:, cols] = jnp.where(lo_q, swap(even), odd)

    @pl.loop(1, nz)
    def _(i):
        dz = dest_of(i)
        q_copy(dz).wait_send()
        rb_copy(dz).wait_send()
        kv_copy(dz).wait_send()
        o_copy(dz).wait_send()

    @pl.loop(0, nz)
    def _(i):
        right_copy(i).wait_send()
        left_copy(i).wait_send()
        half_right(i).wait_send()
        half_left(i).wait_send()

    for d in range(1, X):
        qc_copy(d).wait_send()
        gp_copy(d).wait_send()


def per_device(queries, keys_values, random_blocks, global_blocks, out_proj):
    tokens, width = queries.shape
    bd = tokens // BLK
    nz = lax.axis_size("seq") // X
    head_dim = width // H
    assert nz == H and head_dim == HALF and bd % 2 == 0
    lists = random_blocks.transpose(1, 0, 2).reshape(H, 1, bd * R)
    lists = jnp.pad(lists, ((0, 0), (0, 7), (0, LANES - bd * R)))
    nb = nz * X * bd
    scale2 = 1.4426950408889634 * head_dim ** -0.5
    dma = pltpu.SemaphoreType.DMA
    vm = pl.BlockSpec(memory_space=pltpu.VMEM)
    half_tok = tokens // 2
    ctx = pl.pallas_call(
        functools.partial(kernel, nz, bd, scale2),
        out_shape=jax.ShapeDtypeStruct((tokens, width), BF16),
        in_specs=[pl.BlockSpec(memory_space=pltpu.SMEM), vm, vm, vm],
        out_specs=vm,
        scratch_shapes=[
            pltpu.VMEM((nz, bd // 2, BLK, LANES), BF16),
            pltpu.VMEM((nz, bd, BLK, LANES), BF16),
            pltpu.VMEM((nb + 2, BLK, LANES), BF16),
            pltpu.VMEM((nz, bd // 2, BLK, LANES), BF16),
            pltpu.VMEM((nz, 8, LANES), jnp.int32),
            pltpu.SMEM((nz, 8, LANES), jnp.int32),
            pltpu.VMEM((X, G, BLK, LANES), BF16),
            pltpu.VMEM((X, G * BLK, LANES), F32),
            pltpu.VMEM((G * BLK, LANES), F32),
            pltpu.VMEM((G * BLK, LANES), BF16),
            pltpu.VMEM((nz, half_tok, LANES), BF16),
            pltpu.VMEM((nz, half_tok, LANES), BF16),
            pltpu.VMEM((2, G * BLK, LANES), F32),
        ]
        + [dma((nz,))] * 16
        + [dma((X,))] * 4
        + [dma],
        compiler_params=pltpu.CompilerParams(
            collective_id=0, has_side_effects=True, vmem_limit_bytes=40 * 1024 * 1024
        ),
    )(global_blocks, queries, keys_values, lists)
    weights = lax.all_gather(out_proj, "seq", axis=0, tiled=True)
    return jnp.dot(ctx, weights, preferred_element_type=F32).astype(BF16)


def solution(mesh):
    placed = (
        P(("batch", "seq"), None),
        P(None, ("batch", "seq"), None),
        P(("batch", "seq"), None, None),
        P("batch"),
        P("seq", None),
    )
    return jax.shard_map(
        per_device, mesh=mesh, in_specs=placed, out_specs=P(("batch", "seq"), None), check_vma=False
    )
```

```python
import functools

import jax
import jax.numpy as jnp
from jax import lax
from jax.experimental import pallas as pl
from jax.experimental.pallas import tpu as pltpu
from jax.sharding import PartitionSpec as P

H = 16
BLK = 64
R = 3
X = 4
G = 2
HALF = 64
LANES = 128
MESH = pl.DeviceIdType.MESH
NEG = -1e30
F32 = jnp.float32
BF16 = jnp.bfloat16


def swap(x):
    return pltpu.roll(x.astype(F32), HALF, 1).astype(x.dtype)


def dot_nt(a, b):
    return lax.dot_general(a, b, (((1,), (1,)), ((), ())), preferred_element_type=F32)


def dot_nn(a, b):
    return lax.dot_general(a, b, (((1,), (0,)), ((), ())), preferred_element_type=F32)


def kernel(
    nz, bd, scale2,
    gb_ref, rb_ref, q_hbm, kv_hbm, w_hbm, out_ref,
    q_ref, kv_ref, w_ref, rb_out, ctx_ref, w_all,
    qpack, kvpack, kvf, q_in, rb_in, rb_s, qc_in, gpart, gout, gkv, o_pack, o_in, stat,
    q_send, q_recv, rb_send, rb_recv, kv_send, kv_recv, o_send, o_recv,
    r_send, l_send, fl_recv, fr_recv, ha_send, hb_send, oa_recv, ob_recv,
    wz_send, wz_recv, qc_send, qc_recv, gp_send, gp_recv, wx_send, wx_recv, wb_send, wb_recv, load_sem, rbs_sem,
):
    tok = bd * BLK
    half_tok = tok // 2
    half_bd = bd // 2
    nb = nz * X * bd
    batch = lax.axis_index("batch")
    me = lax.axis_index("seq")
    nk = lax.axis_size("batch")
    cols_k = out_ref.shape[1] // nk
    z = me // X
    x = lax.rem(me, X)
    right = lax.rem(x + 1, X)
    left = lax.rem(x + X - 1, X)

    def dev(zz, xx):
        return (batch, zz * X + xx)

    def remote(src, dst, send, recv, where):
        return pltpu.make_async_remote_copy(
            src_ref=src, dst_ref=dst, send_sem=send, recv_sem=recv, device_id=where, device_id_type=MESH
        )

    def order(i):
        return lax.rem(jnp.where(lax.rem(i, 2) == 1, (i + 1) // 2, nz - i // 2), nz)

    def dest_of(i):
        return lax.rem(z + order(i), nz)

    def src_of(i):
        return lax.rem(z + nz - order(i), nz)

    def rows(zz, xx, first=0, count=None):
        return pl.ds(1 + (zz * X + xx) * bd + first, bd if count is None else count)

    loads = [
        pltpu.make_async_copy(src, dst, load_sem.at[n])
        for n, (src, dst) in enumerate(((q_hbm, q_ref), (kv_hbm, kv_ref), (w_hbm, w_ref)))
    ]
    for load in loads:
        load.start()

    barrier = pltpu.get_barrier_semaphore()

    @pl.loop(1, nz)
    def _(i):
        pl.semaphore_signal(barrier, inc=1, device_id=dev(lax.rem(z + i, nz), x), device_id_type=MESH)

    for d in range(1, X):
        pl.semaphore_signal(barrier, inc=1, device_id=dev(z, lax.rem(x + d, X)), device_id_type=MESH)

    @pl.loop(1, nk)
    def _(i):
        pl.semaphore_signal(barrier, inc=1, device_id=(lax.rem(batch + i, nk), me), device_id_type=MESH)

    lane_l = lax.broadcasted_iota(jnp.int32, (nz, LANES), 1)
    lists = jnp.zeros((nz, LANES), jnp.int32)
    for j in range(bd):
        for r in range(R):
            lists = jnp.where(lane_l == j * R + r, rb_ref[j, :, r:r + 1], lists)
    for h in range(nz):
        rb_out[h] = lists[h:h + 1, :]
    loads[0].wait()

    lo_q = lax.broadcasted_iota(jnp.int32, (half_tok, LANES), 1) < HALF
    for p in range(nz // 2):
        cols = slice(p * LANES, (p + 1) * LANES)
        top, bot = q_ref[:half_tok, cols], q_ref[half_tok:, cols]
        qpack[2 * p] = jnp.where(lo_q, top, swap(bot)).reshape(half_bd, BLK, LANES)
        qpack[2 * p + 1] = jnp.where(lo_q, swap(top), bot).reshape(half_bd, BLK, LANES)

    loads[2].wait()
    for kk in range(nk):
        @pl.when(batch == kk)
        def _():
            w_all[kk, x, z] = w_ref[:, kk * cols_k:(kk + 1) * cols_k]

    pl.semaphore_wait(barrier, nz - 1 + X - 1 + nk - 1)

    def q_copy(dz):
        return remote(qpack.at[dz], q_in.at[z], q_send.at[dz], q_recv.at[z], dev(dz, x))

    def rb_copy(dz):
        return remote(rb_out.at[dz], rb_in.at[z], rb_send.at[dz], rb_recv.at[z], dev(dz, x))

    def wz_copy(dz):
        part = w_all.at[batch, x, z]
        return remote(part, part, wz_send.at[dz], wz_recv.at[z], dev(dz, x))

    def wx_copy(d):
        part = w_all.at[batch, x]
        return remote(part, part, wx_send.at[d], wx_recv.at[x], dev(z, lax.rem(x + d, X)))

    def wb_copy(i):
        to = lax.rem(batch + i, nk)
        part = w_all.at[batch]
        return remote(part, part, wb_send.at[to], wb_recv.at[batch], (to, me))

    def kv_copy(dz):
        return remote(kvpack.at[dz], kvf.at[rows(z, x)], kv_send.at[dz], kv_recv.at[z], dev(dz, x))

    def o_copy(dz):
        return remote(o_pack.at[dz], o_in.at[z], o_send.at[dz], o_recv.at[z], dev(dz, x))

    @pl.loop(1, nz)
    def _(i):
        dz = dest_of(i)
        q_copy(dz).start()
        rb_copy(dz).start()
        wz_copy(dz).start()

    loads[1].wait()
    lo_t = lax.broadcasted_iota(jnp.int32, (tok, LANES), 1) < HALF
    for p in range(nz // 2):
        cols = slice(p * LANES, (p + 1) * LANES)
        keys, vals = kv_ref[0, :, cols], kv_ref[1, :, cols]
        kvpack[2 * p] = jnp.where(lo_t, keys, swap(vals)).reshape(bd, BLK, LANES)
        kvpack[2 * p + 1] = jnp.where(lo_t, swap(keys), vals).reshape(bd, BLK, LANES)

    @pl.loop(1, nz)
    def _(i):
        kv_copy(dest_of(i)).start()

    q_in[z] = qpack[z]
    rb_in[z] = rb_out[z]
    kvf[rows(z, x)] = kvpack[z]
    kvf[0] = jnp.zeros((BLK, LANES), BF16)
    kvf[nb + 1] = jnp.zeros((BLK, LANES), BF16)

    @pl.loop(1, nz)
    def _(i):
        zs = src_of(i)
        remote(qpack.at[zs], q_in.at[zs], q_send.at[zs], q_recv.at[zs], dev(zs, x)).wait_recv()
        remote(rb_out.at[zs], rb_in.at[zs], rb_send.at[zs], rb_recv.at[zs], dev(zs, x)).wait_recv()
        part = w_all.at[batch, x, zs]
        remote(part, part, wz_send.at[zs], wz_recv.at[zs], dev(zs, x)).wait_recv()

    for d in range(1, X):
        wx_copy(d).start()

    to_smem = pltpu.make_async_copy(rb_in, rb_s, rbs_sem)
    to_smem.start()

    lo_b = lax.broadcasted_iota(jnp.int32, (BLK, LANES), 1) < HALF

    def spread(number):
        return jnp.broadcast_to(number, (BLK, LANES))

    for g in range(G):
        block = gb_ref[g]
        within = lax.rem(block, bd)
        tile = q_in[lax.div(block, bd * X), lax.rem(within, half_bd)]
        tile = jnp.where(spread(within) >= half_bd, swap(tile), tile)
        qc_in[x, g] = jnp.where(lo_b, tile, jnp.zeros_like(tile))

    def qc_copy(d):
        return remote(qc_in.at[x], qc_in.at[x], qc_send.at[d], qc_recv.at[x], dev(z, lax.rem(x + d, X)))

    def qc_wait(d):
        xs = lax.rem(x + d, X)
        remote(qc_in.at[xs], qc_in.at[xs], qc_send.at[d], qc_recv.at[xs], dev(z, xs)).wait_recv()

    for d in range(1, X):
        qc_copy(d).start()
    for d in range(1, X):
        qc_wait(d)

    glob_q = jnp.concatenate(
        [qc_in[lax.rem(lax.div(gb_ref[g], bd), X), g] for g in range(G)], axis=0
    )
    gout[...] = jnp.zeros_like(gout)
    stat[0] = jnp.full((G * BLK, LANES), NEG, F32)
    stat[1] = jnp.zeros((G * BLK, LANES), F32)

    def right_copy(zs):
        part = kvf.at[rows(zs, x)]
        return remote(part, part, r_send.at[zs], fl_recv.at[zs], dev(z, right))

    def left_copy(zs):
        part = kvf.at[rows(zs, x)]
        return remote(part, part, l_send.at[zs], fr_recv.at[zs], dev(z, left))

    def from_left(zs):
        part = kvf.at[rows(zs, left)]
        return remote(part, part, r_send.at[zs], fl_recv.at[zs], dev(z, left))

    def from_right(zs):
        part = kvf.at[rows(zs, right)]
        return remote(part, part, l_send.at[zs], fr_recv.at[zs], dev(z, right))

    def half_right(zs):
        part = kvf.at[rows(zs, left, 0, half_bd)]
        return remote(part, part, ha_send.at[zs], oa_recv.at[zs], dev(z, right))

    def half_left(zs):
        part = kvf.at[rows(zs, right, half_bd, half_bd)]
        return remote(part, part, hb_send.at[zs], ob_recv.at[zs], dev(z, left))

    opposite = lax.rem(x + 2, X)

    def half_a(zs):
        part = kvf.at[rows(zs, opposite, 0, half_bd)]
        return remote(part, part, ha_send.at[zs], oa_recv.at[zs], dev(z, left))

    def half_b(zs):
        part = kvf.at[rows(zs, opposite, half_bd, half_bd)]
        return remote(part, part, hb_send.at[zs], ob_recv.at[zs], dev(z, right))

    def pass_on(zs):
        from_left(zs).wait_recv()
        half_right(zs).start()
        from_right(zs).wait_recv()
        half_left(zs).start()

    @pl.loop(0, nz)
    def _(i):
        zs = src_of(i)

        @pl.when(i > 0)
        def _():
            part = kvf.at[rows(zs, x)]
            remote(part, part, kv_send.at[zs], kv_recv.at[zs], dev(zs, x)).wait_recv()

        right_copy(zs).start()
        left_copy(zs).start()
        chunk = kvf[rows(zs, x)].reshape(tok, LANES)
        scores = dot_nt(glob_q, chunk)
        old_max = stat[0]
        new_max = jnp.maximum(old_max, jnp.max(scores, axis=1, keepdims=True))
        shrink = jnp.exp2((old_max - new_max) * scale2)
        weights = jnp.exp2((scores - new_max[:, :1]) * scale2)
        stat[0] = new_max
        stat[1] = stat[1] * shrink + jnp.sum(weights, axis=1, keepdims=True)
        gout[...] = gout[...] * shrink + dot_nn(weights.astype(BF16), chunk)

        @pl.when(i > 0)
        def _():
            pass_on(src_of(i - 1))

        @pl.when(i == 2)
        def _():
            for d in range(1, X):
                xs = lax.rem(x + d, X)
                part = w_all.at[batch, xs]
                remote(part, part, wx_send.at[d], wx_recv.at[xs], dev(z, xs)).wait_recv()

            @pl.loop(1, nk)
            def _(n):
                wb_copy(n).start()

    lane_g = lax.broadcasted_iota(jnp.int32, (G * BLK, LANES), 1)
    gpart[x] = jnp.where(lane_g < HALF // 2, stat[0], jnp.where(lane_g < HALF, stat[1], gout[...]))

    def gp_copy(d):
        return remote(gpart.at[x], gpart.at[x], gp_send.at[d], gp_recv.at[x], dev(z, lax.rem(x + d, X)))

    def gp_wait(d):
        xs = lax.rem(x + d, X)
        remote(gpart.at[xs], gpart.at[xs], gp_send.at[d], gp_recv.at[xs], dev(z, xs)).wait_recv()

    for d in range(1, X):
        gp_copy(d).start()
    pass_on(src_of(nz - 1))

    @pl.loop(0, nz)
    def _(i):
        zs = src_of(i)
        half_a(zs).wait_recv()
        half_b(zs).wait_recv()

    for d in range(1, X):
        gp_wait(d)
    top_max = functools.reduce(jnp.maximum, [gpart[c][:, :1] for c in range(X)])
    glob_total = jnp.zeros((G * BLK, 1), F32)
    glob_acc = jnp.zeros((G * BLK, LANES), F32)
    for c in range(X):
        part = gpart[c]
        factor = jnp.exp2((part[:, :1] - top_max) * scale2)
        glob_total = glob_total + part[:, HALF // 2:HALF // 2 + 1] * factor
        glob_acc = glob_acc + part * factor
    gout[...] = glob_acc / glob_total

    for g in range(G):
        gkv[g * BLK:(g + 1) * BLK, :] = kvf[1 + gb_ref[g]]
    to_smem.wait()

    key_lane = lax.broadcasted_iota(jnp.int32, (BLK, (3 + R + G) * BLK), 1)

    @pl.loop(0, nz)
    def _(n):
        i = nz - 1 - n
        zs = src_of(i)
        packed = q_in[zs].reshape(half_tok, LANES)
        zero = jnp.zeros_like(packed)
        halves = (jnp.where(lo_q, packed, zero), jnp.where(lo_q, swap(packed), zero))
        outs = []
        for j in range(bd):
            block = (zs * X + x) * bd + j
            first = (j % half_bd) * BLK
            qb = halves[j // half_bd][first:first + BLK, :]
            parts = [kvf[block + w] for w in range(3)]
            for r in range(R):
                pick = rb_s[zs, 0, j * R + r]
                parts.append(kvf[1 + pick])
            parts.append(gkv[...])
            keyval = jnp.concatenate(parts, axis=0)
            scores = dot_nt(qb, keyval)
            if j == 0:
                scores = jnp.where((key_lane < BLK) & (block == 0), NEG, scores)
            if j == bd - 1:
                outside = (key_lane >= 2 * BLK) & (key_lane < 3 * BLK) & (block == nb - 1)
                scores = jnp.where(outside, NEG, scores)
            row_max = jnp.max(scores, axis=1, keepdims=True)
            weights = jnp.exp2((scores - row_max) * scale2)
            total = jnp.sum(weights, axis=1, keepdims=True)
            mixed = dot_nn(weights.astype(BF16), keyval) / total
            for g in range(G):
                mixed = jnp.where(spread(gb_ref[g]) == block, gout[g * BLK:(g + 1) * BLK, :], mixed)
            outs.append(mixed)
        low = jnp.concatenate(outs[:half_bd], axis=0)
        high = jnp.concatenate(outs[half_bd:], axis=0)
        o_pack[zs] = jnp.where(lo_q, pltpu.roll(low, HALF, 1), high).astype(BF16)

        @pl.when(i > 0)
        def _():
            o_copy(zs).start()

    o_in[z] = o_pack[z]

    @pl.loop(1, nz)
    def _(i):
        zs = src_of(i)
        remote(o_pack.at[zs], o_in.at[zs], o_send.at[zs], o_recv.at[zs], dev(zs, x)).wait_recv()

    for p in range(nz // 2):
        cols = slice(p * LANES, (p + 1) * LANES)
        even, odd = o_in[2 * p], o_in[2 * p + 1]
        ctx_ref[:half_tok, cols] = jnp.where(lo_q, even, swap(odd))
        ctx_ref[half_tok:, cols] = jnp.where(lo_q, swap(even), odd)

    @pl.loop(1, nz)
    def _(i):
        dz = dest_of(i)
        q_copy(dz).wait_send()
        rb_copy(dz).wait_send()
        wz_copy(dz).wait_send()
        kv_copy(dz).wait_send()
        o_copy(dz).wait_send()

    @pl.loop(0, nz)
    def _(i):
        right_copy(i).wait_send()
        left_copy(i).wait_send()
        half_right(i).wait_send()
        half_left(i).wait_send()

    @pl.loop(1, nk)
    def _(n):
        kk = lax.rem(batch + n, nk)
        part = w_all.at[kk]
        remote(part, part, wb_send.at[kk], wb_recv.at[kk], (kk, me)).wait_recv()

    step = 2 * cols_k

    @pl.loop(0, nk // 2)
    def _(n):
        pair = []
        for kk in (2 * n, 2 * n + 1):
            pair.append(jnp.concatenate([w_all[kk, xx, zz] for zz in range(nz) for xx in range(X)], axis=0))
        product = dot_nn(ctx_ref[...], jnp.concatenate(pair, axis=1))
        out_ref[:, pl.ds(pl.multiple_of(n * step, step), step)] = product.astype(BF16)

    @pl.loop(1, nk)
    def _(n):
        wb_copy(n).wait_send()

    for d in range(1, X):
        wx_copy(d).wait_send()
        qc_copy(d).wait_send()
        gp_copy(d).wait_send()


def per_device(queries, keys_values, random_blocks, global_blocks, out_proj):
    tokens, width = queries.shape
    bd = tokens // BLK
    nz = lax.axis_size("seq") // X
    head_dim = width // H
    assert nz == H and head_dim == HALF and bd % 2 == 0
    nb = nz * X * bd
    scale2 = 1.4426950408889634 * head_dim ** -0.5
    dma = pltpu.SemaphoreType.DMA
    vm = pl.BlockSpec(memory_space=pltpu.VMEM)
    half_tok = tokens // 2
    hbm = pl.BlockSpec(memory_space=pltpu.HBM)
    nk = lax.axis_size("batch")
    w_rows = out_proj.shape[0]
    return pl.pallas_call(
        functools.partial(kernel, nz, bd, scale2),
        out_shape=jax.ShapeDtypeStruct((tokens, width), BF16),
        in_specs=[pl.BlockSpec(memory_space=pltpu.SMEM), vm, hbm, hbm, hbm],
        out_specs=vm,
        scratch_shapes=[
            pltpu.VMEM((tokens, width), BF16),
            pltpu.VMEM((2, tokens, width), BF16),
            pltpu.VMEM((w_rows, width), BF16),
            pltpu.VMEM((nz, 1, LANES), jnp.int32),
            pltpu.VMEM((tokens, width), BF16),
            pltpu.VMEM((nk, X, nz, w_rows, width // nk), BF16),
            pltpu.VMEM((nz, bd // 2, BLK, LANES), BF16),
            pltpu.VMEM((nz, bd, BLK, LANES), BF16),
            pltpu.VMEM((nb + 2, BLK, LANES), BF16),
            pltpu.VMEM((nz, bd // 2, BLK, LANES), BF16),
            pltpu.VMEM((nz, 1, LANES), jnp.int32),
            pltpu.SMEM((nz, 1, LANES), jnp.int32),
            pltpu.VMEM((X, G, BLK, LANES), BF16),
            pltpu.VMEM((X, G * BLK, LANES), F32),
            pltpu.VMEM((G * BLK, LANES), F32),
            pltpu.VMEM((G * BLK, LANES), BF16),
            pltpu.VMEM((nz, half_tok, LANES), BF16),
            pltpu.VMEM((nz, half_tok, LANES), BF16),
            pltpu.VMEM((2, G * BLK, LANES), F32),
        ]
        + [dma((nz,))] * 18
        + [dma((X,))] * 6
        + [dma((nk,))] * 2
        + [dma((3,)), dma],
        compiler_params=pltpu.CompilerParams(
            collective_id=0, has_side_effects=True, vmem_limit_bytes=62 * 1024 * 1024
        ),
    )(global_blocks, random_blocks, queries, keys_values, out_proj)


def solution(mesh):
    placed = (
        P(("batch", "seq"), None),
        P(None, ("batch", "seq"), None),
        P(("batch", "seq"), None, None),
        P("batch"),
        P("seq", None),
    )
    return jax.shard_map(
        per_device, mesh=mesh, in_specs=placed, out_specs=P(("batch", "seq"), None), check_vma=False
    )
```

```python
import functools

import jax
import jax.numpy as jnp
from jax import lax
from jax.experimental import pallas as pl
from jax.experimental.pallas import tpu as pltpu
from jax.sharding import PartitionSpec as P

H = 16
BLK = 64
R = 3
X = 4
G = 2
HALF = 64
LANES = 128
MESH = pl.DeviceIdType.MESH
NEG = -1e30
F32 = jnp.float32
BF16 = jnp.bfloat16


def swap(x):
    return pltpu.roll(x.astype(F32), HALF, 1).astype(x.dtype)


def dot_nt(a, b):
    return lax.dot_general(a, b, (((1,), (1,)), ((), ())), preferred_element_type=F32)


def dot_nn(a, b):
    return lax.dot_general(a, b, (((1,), (0,)), ((), ())), preferred_element_type=F32)


def kernel(
    nz, bd, scale2,
    gb_ref, rb_ref, q_hbm, kv_hbm, w_hbm, out_ref,
    q_ref, kv_ref, w_ref, rb_out, ctx_ref, w_all,
    qpack, kvpack, kvf, q_in, rb_in, rb_s, cand, c_x, c_sum, c_z, c_all, gpart, gout, gkv, o_pack, o_in, stat,
    q_send, q_recv, rb_send, rb_recv, kv_send, kv_recv, o_send, o_recv,
    r_send, l_send, fl_recv, fr_recv, ha_send, hb_send, oa_recv, ob_recv,
    wz_send, wz_recv, cz_send, cz_recv, cx_send, cx_recv, ca_send, gp_send, gp_recv, wx_send, wx_recv, wb_send, wb_recv, load_sem, ca_recv, rbs_sem,
):
    tok = bd * BLK
    half_tok = tok // 2
    half_bd = bd // 2
    nb = nz * X * bd
    batch = lax.axis_index("batch")
    me = lax.axis_index("seq")
    nk = lax.axis_size("batch")
    cols_k = out_ref.shape[1] // nk
    z = me // X
    x = lax.rem(me, X)
    right = lax.rem(x + 1, X)
    left = lax.rem(x + X - 1, X)

    def dev(zz, xx):
        return (batch, zz * X + xx)

    def remote(src, dst, send, recv, where):
        return pltpu.make_async_remote_copy(
            src_ref=src, dst_ref=dst, send_sem=send, recv_sem=recv, device_id=where, device_id_type=MESH
        )

    def order(i):
        return lax.rem(jnp.where(lax.rem(i, 2) == 1, (i + 1) // 2, nz - i // 2), nz)

    def dest_of(i):
        return lax.rem(z + order(i), nz)

    def src_of(i):
        return lax.rem(z + nz - order(i), nz)

    def rows(zz, xx, first=0, count=None):
        return pl.ds(1 + (zz * X + xx) * bd + first, bd if count is None else count)

    loads = [
        pltpu.make_async_copy(src, dst, load_sem.at[n])
        for n, (src, dst) in enumerate(((q_hbm, q_ref), (kv_hbm, kv_ref), (w_hbm, w_ref)))
    ]
    for load in loads:
        load.start()

    barrier = pltpu.get_barrier_semaphore()

    @pl.loop(1, nz)
    def _(i):
        pl.semaphore_signal(barrier, inc=1, device_id=dev(lax.rem(z + i, nz), x), device_id_type=MESH)

    for d in range(1, X):
        pl.semaphore_signal(barrier, inc=1, device_id=dev(z, lax.rem(x + d, X)), device_id_type=MESH)

    @pl.loop(1, nk)
    def _(i):
        pl.semaphore_signal(barrier, inc=1, device_id=(lax.rem(batch + i, nk), me), device_id_type=MESH)

    lane_l = lax.broadcasted_iota(jnp.int32, (nz, LANES), 1)
    lists = jnp.zeros((nz, LANES), jnp.int32)
    for j in range(bd):
        for r in range(R):
            lists = jnp.where(lane_l == j * R + r, rb_ref[j, :, r:r + 1], lists)
    for h in range(nz):
        rb_out[h] = lists[h:h + 1, :]
    loads[0].wait()

    lo_q = lax.broadcasted_iota(jnp.int32, (half_tok, LANES), 1) < HALF
    lo_b = lax.broadcasted_iota(jnp.int32, (BLK, LANES), 1) < HALF
    lo_t = lax.broadcasted_iota(jnp.int32, (tok, LANES), 1) < HALF

    def spread(number):
        return jnp.broadcast_to(number, (BLK, LANES))

    for p in range(nz // 2):
        cols = slice(p * LANES, (p + 1) * LANES)
        tiles = []
        for g in range(G):
            tile = q_ref[lax.rem(gb_ref[g], bd), :, cols]
            tiles.append(jnp.where(spread(lax.div(gb_ref[g], bd)) == me, tile, jnp.zeros_like(tile)))
        cand[2 * p] = jnp.where(lo_b, tiles[0], swap(tiles[1]))
        cand[2 * p + 1] = jnp.where(lo_b, swap(tiles[0]), tiles[1])
    loads[1].wait()
    for p in range(nz // 2):
        cols = slice(p * LANES, (p + 1) * LANES)
        keys, vals = kv_ref[0, :, cols], kv_ref[1, :, cols]
        kvpack[2 * p] = jnp.where(lo_t, keys, swap(vals)).reshape(bd, BLK, LANES)
        kvpack[2 * p + 1] = jnp.where(lo_t, swap(keys), vals).reshape(bd, BLK, LANES)
    loads[2].wait()
    for kk in range(nk):
        @pl.when(batch == kk)
        def _():
            w_all[kk, x, z] = w_ref[:, kk * cols_k:(kk + 1) * cols_k]

    pl.semaphore_wait(barrier, nz - 1 + X - 1 + nk - 1)

    def q_copy(dz):
        return remote(qpack.at[dz], q_in.at[z], q_send.at[dz], q_recv.at[z], dev(dz, x))

    def rb_copy(dz):
        return remote(rb_out.at[dz], rb_in.at[z], rb_send.at[dz], rb_recv.at[z], dev(dz, x))

    def wz_copy(dz):
        part = w_all.at[batch, x, z]
        return remote(part, part, wz_send.at[dz], wz_recv.at[z], dev(dz, x))

    def wx_copy(d):
        part = w_all.at[batch, x]
        return remote(part, part, wx_send.at[d], wx_recv.at[x], dev(z, lax.rem(x + d, X)))

    def wb_copy(i):
        to = lax.rem(batch + i, nk)
        part = w_all.at[batch]
        return remote(part, part, wb_send.at[to], wb_recv.at[batch], (to, me))

    def kv_copy(dz):
        return remote(kvpack.at[dz], kvf.at[rows(z, x)], kv_send.at[dz], kv_recv.at[z], dev(dz, x))

    def o_copy(dz):
        return remote(o_pack.at[dz], o_in.at[z], o_send.at[dz], o_recv.at[z], dev(dz, x))

    hx = nz // X

    def cx_copy(d):
        to = lax.rem(x + d, X)
        return remote(cand.at[pl.ds(to * hx, hx)], c_x.at[x], cx_send.at[d], cx_recv.at[x], dev(z, to))

    def cz_copy(k):
        to = x * hx + k
        return remote(c_sum.at[k], c_z.at[z], cz_send.at[k], cz_recv.at[z], dev(to, x))

    for d in range(1, X):
        cx_copy(d).start()

    @pl.loop(1, nz)
    def _(i):
        dz = dest_of(i)
        rb_copy(dz).start()
        wz_copy(dz).start()

    @pl.loop(1, nz)
    def _(i):
        kv_copy(dest_of(i)).start()

    for p in range(nz // 2):
        cols = slice(p * LANES, (p + 1) * LANES)
        top = q_ref[:half_bd, :, cols].reshape(half_tok, LANES)
        bot = q_ref[half_bd:, :, cols].reshape(half_tok, LANES)
        qpack[2 * p] = jnp.where(lo_q, top, swap(bot)).reshape(half_bd, BLK, LANES)
        qpack[2 * p + 1] = jnp.where(lo_q, swap(top), bot).reshape(half_bd, BLK, LANES)

    c_x[x] = cand[pl.ds(x * hx, hx)]
    for d in range(1, X):
        xs = lax.rem(x + d, X)
        remote(c_x.at[xs], c_x.at[xs], cx_send.at[d], cx_recv.at[xs], dev(z, xs)).wait_recv()
    c_sum[...] = (c_x[0] + c_x[1]) + (c_x[2] + c_x[3])
    for k in range(hx):
        @pl.when(x * hx + k != z)
        def _():
            cz_copy(k).start()

        @pl.when(x * hx + k == z)
        def _():
            c_z[z] = c_sum[k]

    @pl.loop(1, nz)
    def _(n):
        q_copy(dest_of(nz - n)).start()

    q_in[z] = qpack[z]
    rb_in[z] = rb_out[z]
    kvf[rows(z, x)] = kvpack[z]
    kvf[0] = jnp.zeros((BLK, LANES), BF16)
    kvf[nb + 1] = jnp.zeros((BLK, LANES), BF16)

    def right_copy(zs):
        part = kvf.at[rows(zs, x)]
        return remote(part, part, r_send.at[zs], fl_recv.at[zs], dev(z, right))

    def left_copy(zs):
        part = kvf.at[rows(zs, x)]
        return remote(part, part, l_send.at[zs], fr_recv.at[zs], dev(z, left))

    def from_left(zs):
        part = kvf.at[rows(zs, left)]
        return remote(part, part, r_send.at[zs], fl_recv.at[zs], dev(z, left))

    def from_right(zs):
        part = kvf.at[rows(zs, right)]
        return remote(part, part, l_send.at[zs], fr_recv.at[zs], dev(z, right))

    def half_right(zs):
        part = kvf.at[rows(zs, left, 0, half_bd)]
        return remote(part, part, ha_send.at[zs], oa_recv.at[zs], dev(z, right))

    def half_left(zs):
        part = kvf.at[rows(zs, right, half_bd, half_bd)]
        return remote(part, part, hb_send.at[zs], ob_recv.at[zs], dev(z, left))

    opposite = lax.rem(x + 2, X)

    def half_a(zs):
        part = kvf.at[rows(zs, opposite, 0, half_bd)]
        return remote(part, part, ha_send.at[zs], oa_recv.at[zs], dev(z, left))

    def half_b(zs):
        part = kvf.at[rows(zs, opposite, half_bd, half_bd)]
        return remote(part, part, hb_send.at[zs], ob_recv.at[zs], dev(z, right))

    def pass_on(zs):
        from_left(zs).wait_recv()
        half_right(zs).start()
        from_right(zs).wait_recv()
        half_left(zs).start()

    @pl.loop(0, nz)
    def _(i):
        zs = src_of(i)

        @pl.when(i > 0)
        def _():
            part = kvf.at[rows(zs, x)]
            remote(part, part, kv_send.at[zs], kv_recv.at[zs], dev(zs, x)).wait_recv()

        right_copy(zs).start()
        left_copy(zs).start()

        @pl.when(i > 0)
        def _():
            pass_on(src_of(i - 1))

        @pl.when(i == nz // 5)
        def _():
            @pl.loop(1, nz)
            def _(n):
                zw = src_of(n)
                part = w_all.at[batch, x, zw]
                remote(part, part, wz_send.at[zw], wz_recv.at[zw], dev(zw, x)).wait_recv()

            for d in range(1, X):
                wx_copy(d).start()

        @pl.when(i == 3 * nz // 8)
        def _():
            for d in range(1, X):
                xs = lax.rem(x + d, X)
                part = w_all.at[batch, xs]
                remote(part, part, wx_send.at[d], wx_recv.at[xs], dev(z, xs)).wait_recv()

            @pl.loop(1, nk)
            def _(n):
                wb_copy(n).start()

    pass_on(src_of(nz - 1))

    @pl.loop(1, nz)
    def _(i):
        zs = src_of(i)
        remote(rb_out.at[zs], rb_in.at[zs], rb_send.at[zs], rb_recv.at[zs], dev(zs, x)).wait_recv()

    to_smem = pltpu.make_async_copy(rb_in, rb_s, rbs_sem)
    to_smem.start()

    holder = z // hx

    def ca_copy(d):
        to = lax.rem(x + d, X)
        return remote(c_all, c_all, ca_send.at[d], ca_recv, dev(z, to))

    @pl.when(x == holder)
    def _():
        @pl.loop(1, nz)
        def _(n):
            zs = src_of(n)
            remote(c_z.at[zs], c_z.at[zs], cz_send.at[0], cz_recv.at[zs], dev(zs, x)).wait_recv()

        total = c_z[0]
        for zz in range(1, nz):
            total = total + c_z[zz]
        c_all[...] = total
        for d in range(1, X):
            ca_copy(d).start()

    @pl.when(x != holder)
    def _():
        remote(c_all, c_all, ca_send.at[0], ca_recv, dev(z, holder)).wait_recv()

    both = c_all[...]
    glob_q = jnp.concatenate(
        [jnp.where(lo_b, both, jnp.zeros_like(both)), jnp.where(lo_b, swap(both), jnp.zeros_like(both))], axis=0
    )
    gout[...] = jnp.zeros_like(gout)
    stat[0] = jnp.full((G * BLK, LANES), NEG, F32)
    stat[1] = jnp.zeros((G * BLK, LANES), F32)

    @pl.loop(0, nz // 2)
    def _(n):
        chunk = jnp.concatenate([kvf[rows(2 * n + k, x)].reshape(tok, LANES) for k in range(2)], axis=0)
        scores = dot_nt(glob_q, chunk)
        old_max = stat[0]
        new_max = jnp.maximum(old_max, jnp.max(scores, axis=1, keepdims=True))
        shrink = jnp.exp2((old_max - new_max) * scale2)
        weights = jnp.exp2((scores - new_max[:, :1]) * scale2)
        stat[0] = new_max
        stat[1] = stat[1] * shrink + jnp.sum(weights, axis=1, keepdims=True)
        gout[...] = gout[...] * shrink + dot_nn(weights.astype(BF16), chunk)

    lane_g = lax.broadcasted_iota(jnp.int32, (G * BLK, LANES), 1)
    gpart[x] = jnp.where(lane_g < HALF // 2, stat[0], jnp.where(lane_g < HALF, stat[1], gout[...]))

    def gp_copy(d):
        return remote(gpart.at[x], gpart.at[x], gp_send.at[d], gp_recv.at[x], dev(z, lax.rem(x + d, X)))

    def gp_wait(d):
        xs = lax.rem(x + d, X)
        remote(gpart.at[xs], gpart.at[xs], gp_send.at[d], gp_recv.at[xs], dev(z, xs)).wait_recv()

    for d in range(1, X):
        gp_copy(d).start()

    @pl.loop(0, nz)
    def _(i):
        zs = src_of(i)
        half_a(zs).wait_recv()
        half_b(zs).wait_recv()

    for d in range(1, X):
        gp_wait(d)
    top_max = functools.reduce(jnp.maximum, [gpart[c][:, :1] for c in range(X)])
    glob_total = jnp.zeros((G * BLK, 1), F32)
    glob_acc = jnp.zeros((G * BLK, LANES), F32)
    for c in range(X):
        part = gpart[c]
        factor = jnp.exp2((part[:, :1] - top_max) * scale2)
        glob_total = glob_total + part[:, HALF // 2:HALF // 2 + 1] * factor
        glob_acc = glob_acc + part * factor
    gout[...] = glob_acc / glob_total

    for g in range(G):
        gkv[g * BLK:(g + 1) * BLK, :] = kvf[1 + gb_ref[g]]
    to_smem.wait()

    key_lane = lax.broadcasted_iota(jnp.int32, (BLK, (3 + R + G) * BLK), 1)

    @pl.loop(0, nz)
    def _(n):
        i = nz - 1 - n
        zs = src_of(i)

        @pl.when(i > 0)
        def _():
            remote(qpack.at[zs], q_in.at[zs], q_send.at[zs], q_recv.at[zs], dev(zs, x)).wait_recv()

        packed = q_in[zs].reshape(half_tok, LANES)
        zero = jnp.zeros_like(packed)
        halves = (jnp.where(lo_q, packed, zero), jnp.where(lo_q, swap(packed), zero))
        outs = []
        for j in range(bd):
            block = (zs * X + x) * bd + j
            first = (j % half_bd) * BLK
            qb = halves[j // half_bd][first:first + BLK, :]
            parts = [kvf[block + w] for w in range(3)]
            for r in range(R):
                pick = rb_s[zs, 0, j * R + r]
                parts.append(kvf[1 + pick])
            parts.append(gkv[...])
            keyval = jnp.concatenate(parts, axis=0)
            scores = dot_nt(qb, keyval)
            if j == 0:
                scores = jnp.where((key_lane < BLK) & (block == 0), NEG, scores)
            if j == bd - 1:
                outside = (key_lane >= 2 * BLK) & (key_lane < 3 * BLK) & (block == nb - 1)
                scores = jnp.where(outside, NEG, scores)
            row_max = jnp.max(scores, axis=1, keepdims=True)
            weights = jnp.exp2((scores - row_max) * scale2)
            total = jnp.sum(weights, axis=1, keepdims=True)
            mixed = dot_nn(weights.astype(BF16), keyval) / total
            for g in range(G):
                mixed = jnp.where(spread(gb_ref[g]) == block, gout[g * BLK:(g + 1) * BLK, :], mixed)
            outs.append(mixed)
        low = jnp.concatenate(outs[:half_bd], axis=0)
        high = jnp.concatenate(outs[half_bd:], axis=0)
        o_pack[zs] = jnp.where(lo_q, pltpu.roll(low, HALF, 1), high).astype(BF16)

        @pl.when(i > 0)
        def _():
            o_copy(zs).start()

    o_in[z] = o_pack[z]

    @pl.loop(1, nz)
    def _(i):
        zs = src_of(i)
        remote(o_pack.at[zs], o_in.at[zs], o_send.at[zs], o_recv.at[zs], dev(zs, x)).wait_recv()

    for p in range(nz // 2):
        cols = slice(p * LANES, (p + 1) * LANES)
        even, odd = o_in[2 * p], o_in[2 * p + 1]
        ctx_ref[:half_tok, cols] = jnp.where(lo_q, even, swap(odd))
        ctx_ref[half_tok:, cols] = jnp.where(lo_q, swap(even), odd)

    @pl.loop(1, nz)
    def _(i):
        dz = dest_of(i)
        q_copy(dz).wait_send()
        rb_copy(dz).wait_send()
        wz_copy(dz).wait_send()
        kv_copy(dz).wait_send()
        o_copy(dz).wait_send()

    @pl.loop(0, nz)
    def _(i):
        right_copy(i).wait_send()
        left_copy(i).wait_send()
        half_right(i).wait_send()
        half_left(i).wait_send()

    @pl.loop(1, nk)
    def _(n):
        kk = lax.rem(batch + n, nk)
        part = w_all.at[kk]
        remote(part, part, wb_send.at[kk], wb_recv.at[kk], (kk, me)).wait_recv()

    step = 2 * cols_k

    @pl.loop(0, nk // 2)
    def _(n):
        pair = []
        for kk in (2 * n, 2 * n + 1):
            pair.append(jnp.concatenate([w_all[kk, xx, zz] for zz in range(nz) for xx in range(X)], axis=0))
        product = dot_nn(ctx_ref[...], jnp.concatenate(pair, axis=1))
        out_ref[:, pl.ds(pl.multiple_of(n * step, step), step)] = product.astype(BF16)

    @pl.loop(1, nk)
    def _(n):
        wb_copy(n).wait_send()

    for d in range(1, X):
        wx_copy(d).wait_send()
        cx_copy(d).wait_send()
        gp_copy(d).wait_send()

    @pl.when(x == holder)
    def _():
        for d in range(1, X):
            ca_copy(d).wait_send()

    for k in range(hx):
        @pl.when(x * hx + k != z)
        def _():
            cz_copy(k).wait_send()


def per_device(queries, keys_values, random_blocks, global_blocks, out_proj):
    tokens, width = queries.shape
    bd = tokens // BLK
    nz = lax.axis_size("seq") // X
    head_dim = width // H
    assert nz == H and head_dim == HALF and bd % 2 == 0
    nb = nz * X * bd
    scale2 = 1.4426950408889634 * head_dim ** -0.5
    dma = pltpu.SemaphoreType.DMA
    vm = pl.BlockSpec(memory_space=pltpu.VMEM)
    half_tok = tokens // 2
    hbm = pl.BlockSpec(memory_space=pltpu.HBM)
    nk = lax.axis_size("batch")
    w_rows = out_proj.shape[0]
    return pl.pallas_call(
        functools.partial(kernel, nz, bd, scale2),
        out_shape=jax.ShapeDtypeStruct((tokens, width), BF16),
        in_specs=[pl.BlockSpec(memory_space=pltpu.SMEM), vm, hbm, hbm, hbm],
        out_specs=vm,
        scratch_shapes=[
            pltpu.VMEM((bd, BLK, width), BF16),
            pltpu.VMEM((2, tokens, width), BF16),
            pltpu.VMEM((w_rows, width), BF16),
            pltpu.VMEM((nz, 1, LANES), jnp.int32),
            pltpu.VMEM((tokens, width), BF16),
            pltpu.VMEM((nk, X, nz, w_rows, width // nk), BF16),
            pltpu.VMEM((nz, bd // 2, BLK, LANES), BF16),
            pltpu.VMEM((nz, bd, BLK, LANES), BF16),
            pltpu.VMEM((nb + 2, BLK, LANES), BF16),
            pltpu.VMEM((nz, bd // 2, BLK, LANES), BF16),
            pltpu.VMEM((nz, 1, LANES), jnp.int32),
            pltpu.SMEM((nz, 1, LANES), jnp.int32),
            pltpu.VMEM((nz, BLK, LANES), BF16),
            pltpu.VMEM((X, nz // X, BLK, LANES), BF16),
            pltpu.VMEM((nz // X, BLK, LANES), BF16),
            pltpu.VMEM((nz, BLK, LANES), BF16),
            pltpu.VMEM((BLK, LANES), BF16),
            pltpu.VMEM((X, G * BLK, LANES), F32),
            pltpu.VMEM((G * BLK, LANES), F32),
            pltpu.VMEM((G * BLK, LANES), BF16),
            pltpu.VMEM((nz, half_tok, LANES), BF16),
            pltpu.VMEM((nz, half_tok, LANES), BF16),
            pltpu.VMEM((2, G * BLK, LANES), F32),
        ]
        + [dma((nz,))] * 20
        + [dma((X,))] * 7
        + [dma((nk,))] * 2
        + [dma((3,)), dma, dma],
        compiler_params=pltpu.CompilerParams(
            collective_id=0, has_side_effects=True, vmem_limit_bytes=62 * 1024 * 1024
        ),
    )(global_blocks, random_blocks, queries.reshape(bd, BLK, width), keys_values, out_proj)


def solution(mesh):
    placed = (
        P(("batch", "seq"), None),
        P(None, ("batch", "seq"), None),
        P(("batch", "seq"), None, None),
        P("batch"),
        P("seq", None),
    )
    return jax.shard_map(
        per_device, mesh=mesh, in_specs=placed, out_specs=P(("batch", "seq"), None), check_vma=False
    )
```

```python
import functools

import jax
import jax.numpy as jnp
from jax import lax
from jax.experimental import pallas as pl
from jax.experimental.pallas import tpu as pltpu
from jax.sharding import PartitionSpec as P

H = 16
BLK = 64
R = 3
X = 4
G = 2
HALF = 64
LANES = 128
MESH = pl.DeviceIdType.MESH
NEG = -1e30
F32 = jnp.float32
BF16 = jnp.bfloat16


def swap(x):
    return pltpu.roll(x.astype(F32), HALF, 1).astype(x.dtype)


def dot_nt(a, b):
    return lax.dot_general(a, b, (((1,), (1,)), ((), ())), preferred_element_type=F32)


def dot_nn(a, b):
    return lax.dot_general(a, b, (((1,), (0,)), ((), ())), preferred_element_type=F32)


def kernel(
    nz, bd, scale2,
    gb_ref, rb_ref, q_hbm, kv_hbm, w_hbm, out_ref,
    q_ref, kv_ref, w_ref, rb_out, acc, w_all,
    qpack, kvpack, kvf, q_in, rb_in, rb_s, cand, c_x, c_sum, c_z, c_all, gpart, gout, gkv, o_pack, o_in, stat,
    q_send, q_recv, rb_send, rb_recv, kv_send, kv_recv, o_send, o_recv,
    r_send, l_send, fl_recv, fr_recv, ha_send, hb_send, oa_recv, ob_recv,
    wz_send, wz_recv, cz_send, cz_recv, cx_send, cx_recv, ca_send, gp_send, gp_recv, wx_send, wx_recv, wb_send, wb_recv, load_sem, ca_recv, rbs_sem,
):
    tok = bd * BLK
    half_tok = tok // 2
    half_bd = bd // 2
    nb = nz * X * bd
    batch = lax.axis_index("batch")
    me = lax.axis_index("seq")
    nk = lax.axis_size("batch")
    cols_k = out_ref.shape[1] // nk
    z = me // X
    x = lax.rem(me, X)
    right = lax.rem(x + 1, X)
    left = lax.rem(x + X - 1, X)

    def dev(zz, xx):
        return (batch, zz * X + xx)

    def remote(src, dst, send, recv, where):
        return pltpu.make_async_remote_copy(
            src_ref=src, dst_ref=dst, send_sem=send, recv_sem=recv, device_id=where, device_id_type=MESH
        )

    def order(i):
        return lax.rem(jnp.where(lax.rem(i, 2) == 1, (i + 1) // 2, nz - i // 2), nz)

    def dest_of(i):
        return lax.rem(z + order(i), nz)

    def src_of(i):
        return lax.rem(z + nz - order(i), nz)

    def rows(zz, xx, first=0, count=None):
        return pl.ds(1 + (zz * X + xx) * bd + first, bd if count is None else count)

    loads = [
        pltpu.make_async_copy(src, dst, load_sem.at[n])
        for n, (src, dst) in enumerate(((q_hbm, q_ref), (kv_hbm, kv_ref), (w_hbm, w_ref)))
    ]
    for load in loads:
        load.start()

    barrier = pltpu.get_barrier_semaphore()

    @pl.loop(1, nz)
    def _(i):
        pl.semaphore_signal(barrier, inc=1, device_id=dev(lax.rem(z + i, nz), x), device_id_type=MESH)

    for d in range(1, X):
        pl.semaphore_signal(barrier, inc=1, device_id=dev(z, lax.rem(x + d, X)), device_id_type=MESH)

    @pl.loop(1, nk)
    def _(i):
        pl.semaphore_signal(barrier, inc=1, device_id=(lax.rem(batch + i, nk), me), device_id_type=MESH)

    lane_l = lax.broadcasted_iota(jnp.int32, (nz, LANES), 1)
    lists = jnp.zeros((nz, LANES), jnp.int32)
    for j in range(bd):
        for r in range(R):
            lists = jnp.where(lane_l == j * R + r, rb_ref[j, :, r:r + 1], lists)
    for h in range(nz):
        rb_out[h] = lists[h:h + 1, :]
    loads[0].wait()

    lo_q = lax.broadcasted_iota(jnp.int32, (half_tok, LANES), 1) < HALF
    lo_b = lax.broadcasted_iota(jnp.int32, (BLK, LANES), 1) < HALF
    lo_t = lax.broadcasted_iota(jnp.int32, (tok, LANES), 1) < HALF

    def spread(number):
        return jnp.broadcast_to(number, (BLK, LANES))

    for p in range(nz // 2):
        cols = slice(p * LANES, (p + 1) * LANES)
        tiles = []
        for g in range(G):
            tile = q_ref[lax.rem(gb_ref[g], bd), :, cols]
            tiles.append(jnp.where(spread(lax.div(gb_ref[g], bd)) == me, tile, jnp.zeros_like(tile)))
        cand[2 * p] = jnp.where(lo_b, tiles[0], swap(tiles[1]))
        cand[2 * p + 1] = jnp.where(lo_b, swap(tiles[0]), tiles[1])
    loads[1].wait()
    for p in range(nz // 2):
        cols = slice(p * LANES, (p + 1) * LANES)
        keys, vals = kv_ref[0, :, cols], kv_ref[1, :, cols]
        kvpack[2 * p] = jnp.where(lo_t, keys, swap(vals)).reshape(bd, BLK, LANES)
        kvpack[2 * p + 1] = jnp.where(lo_t, swap(keys), vals).reshape(bd, BLK, LANES)
    loads[2].wait()
    for kk in range(nk):
        @pl.when(batch == kk)
        def _():
            w_all[kk, x, z] = w_ref[:, kk * cols_k:(kk + 1) * cols_k]

    pl.semaphore_wait(barrier, nz - 1 + X - 1 + nk - 1)

    def q_copy(dz):
        return remote(qpack.at[dz], q_in.at[z], q_send.at[dz], q_recv.at[z], dev(dz, x))

    def rb_copy(dz):
        return remote(rb_out.at[dz], rb_in.at[z], rb_send.at[dz], rb_recv.at[z], dev(dz, x))

    def wz_copy(dz):
        part = w_all.at[batch, x, z]
        return remote(part, part, wz_send.at[dz], wz_recv.at[z], dev(dz, x))

    def wx_copy(d):
        part = w_all.at[batch, x]
        return remote(part, part, wx_send.at[d], wx_recv.at[x], dev(z, lax.rem(x + d, X)))

    def wb_copy(i):
        to = lax.rem(batch + i, nk)
        part = w_all.at[batch]
        return remote(part, part, wb_send.at[to], wb_recv.at[batch], (to, me))

    def kv_copy(dz):
        return remote(kvpack.at[dz], kvf.at[rows(z, x)], kv_send.at[dz], kv_recv.at[z], dev(dz, x))

    def o_copy(dz):
        return remote(o_pack.at[dz], o_in.at[z], o_send.at[dz], o_recv.at[z], dev(dz, x))

    hx = nz // X

    def cx_copy(d):
        to = lax.rem(x + d, X)
        return remote(cand.at[pl.ds(to * hx, hx)], c_x.at[x], cx_send.at[d], cx_recv.at[x], dev(z, to))

    def cz_copy(k):
        to = x * hx + k
        return remote(c_sum.at[k], c_z.at[z], cz_send.at[k], cz_recv.at[z], dev(to, x))

    for d in range(1, X):
        cx_copy(d).start()

    @pl.loop(1, nz)
    def _(i):
        dz = dest_of(i)
        rb_copy(dz).start()
        wz_copy(dz).start()

    @pl.loop(1, nz // 2 - 1)
    def _(i):
        kv_copy(dest_of(i)).start()

    c_x[x] = cand[pl.ds(x * hx, hx)]
    for d in range(1, X):
        xs = lax.rem(x + d, X)
        remote(c_x.at[xs], c_x.at[xs], cx_send.at[d], cx_recv.at[xs], dev(z, xs)).wait_recv()
    c_sum[...] = (c_x[0] + c_x[1]) + (c_x[2] + c_x[3])
    for k in range(hx):
        @pl.when(x * hx + k != z)
        def _():
            cz_copy(k).start()

        @pl.when(x * hx + k == z)
        def _():
            c_z[z] = c_sum[k]

    @pl.loop(nz // 2 - 1, nz)
    def _(i):
        kv_copy(dest_of(i)).start()

    for p in range(nz // 2):
        cols = slice(p * LANES, (p + 1) * LANES)
        top = q_ref[:half_bd, :, cols].reshape(half_tok, LANES)
        bot = q_ref[half_bd:, :, cols].reshape(half_tok, LANES)
        qpack[2 * p] = jnp.where(lo_q, top, swap(bot)).reshape(half_bd, BLK, LANES)
        qpack[2 * p + 1] = jnp.where(lo_q, swap(top), bot).reshape(half_bd, BLK, LANES)

    @pl.loop(1, nz)
    def _(n):
        q_copy(dest_of(nz - n)).start()

    q_in[z] = qpack[z]
    rb_in[z] = rb_out[z]
    kvf[rows(z, x)] = kvpack[z]
    kvf[0] = jnp.zeros((BLK, LANES), BF16)
    kvf[nb + 1] = jnp.zeros((BLK, LANES), BF16)

    def right_copy(zs):
        part = kvf.at[rows(zs, x)]
        return remote(part, part, r_send.at[zs], fl_recv.at[zs], dev(z, right))

    def left_copy(zs):
        part = kvf.at[rows(zs, x)]
        return remote(part, part, l_send.at[zs], fr_recv.at[zs], dev(z, left))

    def from_left(zs):
        part = kvf.at[rows(zs, left)]
        return remote(part, part, r_send.at[zs], fl_recv.at[zs], dev(z, left))

    def from_right(zs):
        part = kvf.at[rows(zs, right)]
        return remote(part, part, l_send.at[zs], fr_recv.at[zs], dev(z, right))

    def half_right(zs):
        part = kvf.at[rows(zs, left, 0, half_bd)]
        return remote(part, part, ha_send.at[zs], oa_recv.at[zs], dev(z, right))

    def half_left(zs):
        part = kvf.at[rows(zs, right, half_bd, half_bd)]
        return remote(part, part, hb_send.at[zs], ob_recv.at[zs], dev(z, left))

    opposite = lax.rem(x + 2, X)

    def half_a(zs):
        part = kvf.at[rows(zs, opposite, 0, half_bd)]
        return remote(part, part, ha_send.at[zs], oa_recv.at[zs], dev(z, left))

    def half_b(zs):
        part = kvf.at[rows(zs, opposite, half_bd, half_bd)]
        return remote(part, part, hb_send.at[zs], ob_recv.at[zs], dev(z, right))

    holder = z // hx

    def ca_copy(d):
        to = lax.rem(x + d, X)
        return remote(c_all, c_all, ca_send.at[d], ca_recv, dev(z, to))

    gout[...] = jnp.zeros_like(gout)
    stat[0] = jnp.full((G * BLK, LANES), NEG, F32)
    stat[1] = jnp.zeros((G * BLK, LANES), F32)

    def pass_on(zs):
        from_left(zs).wait_recv()
        half_right(zs).start()
        from_right(zs).wait_recv()
        half_left(zs).start()

    @pl.loop(0, nz)
    def _(i):
        zs = src_of(i)

        @pl.when(i > 0)
        def _():
            part = kvf.at[rows(zs, x)]
            remote(part, part, kv_send.at[zs], kv_recv.at[zs], dev(zs, x)).wait_recv()

        right_copy(zs).start()
        left_copy(zs).start()

        @pl.when(i == nz // 2)
        def _():
            @pl.when(x == holder)
            def _():
                @pl.loop(1, nz)
                def _(n):
                    zs = src_of(n)
                    remote(c_z.at[zs], c_z.at[zs], cz_send.at[0], cz_recv.at[zs], dev(zs, x)).wait_recv()

                total = c_z[0]
                for zz in range(1, nz):
                    total = total + c_z[zz]
                c_all[...] = total
                for d in range(1, X):
                    ca_copy(d).start()

            @pl.when(x != holder)
            def _():
                remote(c_all, c_all, ca_send.at[0], ca_recv, dev(z, holder)).wait_recv()

        @pl.when(i >= nz // 2)
        def _():
            n = i - nz // 2
            both = c_all[...]
            glob_q = jnp.concatenate(
                [jnp.where(lo_b, both, jnp.zeros_like(both)), jnp.where(lo_b, swap(both), jnp.zeros_like(both))], axis=0
            )
            chunk = jnp.concatenate([kvf[rows(src_of(2 * n + k), x)].reshape(tok, LANES) for k in range(2)], axis=0)
            scores = dot_nt(glob_q, chunk)
            old_max = stat[0]
            new_max = jnp.maximum(old_max, jnp.max(scores, axis=1, keepdims=True))
            shrink = jnp.exp2((old_max - new_max) * scale2)
            weights = jnp.exp2((scores - new_max[:, :1]) * scale2)
            stat[0] = new_max
            stat[1] = stat[1] * shrink + jnp.sum(weights, axis=1, keepdims=True)
            gout[...] = gout[...] * shrink + dot_nn(weights.astype(BF16), chunk)


        @pl.when(i > 0)
        def _():
            pass_on(src_of(i - 1))

        @pl.when(i == nz // 5)
        def _():
            @pl.loop(1, nz)
            def _(n):
                zw = src_of(n)
                part = w_all.at[batch, x, zw]
                remote(part, part, wz_send.at[zw], wz_recv.at[zw], dev(zw, x)).wait_recv()

            for d in range(1, X):
                wx_copy(d).start()

        @pl.when(i == 3 * nz // 8)
        def _():
            for d in range(1, X):
                xs = lax.rem(x + d, X)
                part = w_all.at[batch, xs]
                remote(part, part, wx_send.at[d], wx_recv.at[xs], dev(z, xs)).wait_recv()

            @pl.loop(1, nk)
            def _(n):
                wb_copy(n).start()

    lane_g = lax.broadcasted_iota(jnp.int32, (G * BLK, LANES), 1)
    gpart[x] = jnp.where(lane_g < HALF // 2, stat[0], jnp.where(lane_g < HALF, stat[1], gout[...]))

    def gp_copy(d):
        return remote(gpart.at[x], gpart.at[x], gp_send.at[d], gp_recv.at[x], dev(z, lax.rem(x + d, X)))

    def gp_wait(d):
        xs = lax.rem(x + d, X)
        remote(gpart.at[xs], gpart.at[xs], gp_send.at[d], gp_recv.at[xs], dev(z, xs)).wait_recv()

    for d in range(1, X):
        gp_copy(d).start()
    pass_on(src_of(nz - 1))

    @pl.loop(1, nz)
    def _(i):
        zs = src_of(i)
        remote(rb_out.at[zs], rb_in.at[zs], rb_send.at[zs], rb_recv.at[zs], dev(zs, x)).wait_recv()

    to_smem = pltpu.make_async_copy(rb_in, rb_s, rbs_sem)
    to_smem.start()


    @pl.loop(0, nz)
    def _(i):
        zs = src_of(i)
        half_a(zs).wait_recv()
        half_b(zs).wait_recv()

    for d in range(1, X):
        gp_wait(d)
    top_max = functools.reduce(jnp.maximum, [gpart[c][:, :1] for c in range(X)])
    glob_total = jnp.zeros((G * BLK, 1), F32)
    glob_acc = jnp.zeros((G * BLK, LANES), F32)
    for c in range(X):
        part = gpart[c]
        factor = jnp.exp2((part[:, :1] - top_max) * scale2)
        glob_total = glob_total + part[:, HALF // 2:HALF // 2 + 1] * factor
        glob_acc = glob_acc + part * factor
    gout[...] = glob_acc / glob_total

    for g in range(G):
        gkv[g * BLK:(g + 1) * BLK, :] = kvf[1 + gb_ref[g]]
    to_smem.wait()

    key_lane = lax.broadcasted_iota(jnp.int32, (BLK, (3 + R + G) * BLK), 1)

    @pl.loop(0, nz)
    def _(n):
        i = nz - 1 - n
        zs = src_of(i)

        @pl.when(i > 0)
        def _():
            remote(qpack.at[zs], q_in.at[zs], q_send.at[zs], q_recv.at[zs], dev(zs, x)).wait_recv()

        packed = q_in[zs].reshape(half_tok, LANES)
        zero = jnp.zeros_like(packed)
        halves = (jnp.where(lo_q, packed, zero), jnp.where(lo_q, swap(packed), zero))
        outs = []
        for j in range(bd):
            block = (zs * X + x) * bd + j
            first = (j % half_bd) * BLK
            qb = halves[j // half_bd][first:first + BLK, :]
            parts = [kvf[block + w] for w in range(3)]
            for r in range(R):
                pick = rb_s[zs, 0, j * R + r]
                parts.append(kvf[1 + pick])
            parts.append(gkv[...])
            keyval = jnp.concatenate(parts, axis=0)
            scores = dot_nt(qb, keyval)
            if j == 0:
                scores = jnp.where((key_lane < BLK) & (block == 0), NEG, scores)
            if j == bd - 1:
                outside = (key_lane >= 2 * BLK) & (key_lane < 3 * BLK) & (block == nb - 1)
                scores = jnp.where(outside, NEG, scores)
            row_max = jnp.max(scores, axis=1, keepdims=True)
            weights = jnp.exp2((scores - row_max) * scale2)
            total = jnp.sum(weights, axis=1, keepdims=True)
            mixed = dot_nn(weights.astype(BF16), keyval) / total
            for g in range(G):
                mixed = jnp.where(spread(gb_ref[g]) == block, gout[g * BLK:(g + 1) * BLK, :], mixed)
            outs.append(mixed)
        low = jnp.concatenate(outs[:half_bd], axis=0)
        high = jnp.concatenate(outs[half_bd:], axis=0)
        o_pack[zs] = jnp.where(lo_q, pltpu.roll(low, HALF, 1), high).astype(BF16)

        @pl.when(i > 0)
        def _():
            o_copy(zs).start()

    o_in[z] = o_pack[z]

    @pl.loop(1, nk)
    def _(n):
        kk = lax.rem(batch + n, nk)
        part = w_all.at[kk]
        remote(part, part, wb_send.at[kk], wb_recv.at[kk], (kk, me)).wait_recv()

    acc[...] = jnp.zeros_like(acc)

    def o_wait(h):
        remote(o_pack.at[h], o_in.at[h], o_send.at[h], o_recv.at[h], dev(h, x)).wait_recv()

    def weight_rows(h):
        parts = [jnp.concatenate([w_all[kk, xx, h] for xx in range(X)], axis=0) for kk in range(nk)]
        return jnp.concatenate(parts, axis=1)

    @pl.loop(0, nz // 2)
    def _(n):
        away = nz // 2 - n
        head_a = lax.rem(z + away, nz)
        head_b = jnp.where(n == 0, z, lax.rem(z + nz - away, nz))
        o_wait(head_a)

        @pl.when(n > 0)
        def _():
            o_wait(head_b)

        one, two = o_in[head_a], o_in[head_b]
        context = jnp.concatenate([jnp.where(lo_q, one, swap(two)), jnp.where(lo_q, swap(one), two)], axis=0)
        acc[...] += dot_nn(context, jnp.concatenate([weight_rows(head_a), weight_rows(head_b)], axis=0))

    out_ref[...] = acc[...].astype(BF16)

    @pl.loop(1, nz)
    def _(i):
        dz = dest_of(i)
        q_copy(dz).wait_send()
        rb_copy(dz).wait_send()
        wz_copy(dz).wait_send()
        kv_copy(dz).wait_send()
        o_copy(dz).wait_send()

    @pl.loop(0, nz)
    def _(i):
        right_copy(i).wait_send()
        left_copy(i).wait_send()
        half_right(i).wait_send()
        half_left(i).wait_send()

    @pl.loop(1, nk)
    def _(n):
        wb_copy(n).wait_send()

    for d in range(1, X):
        wx_copy(d).wait_send()
        cx_copy(d).wait_send()
        gp_copy(d).wait_send()

    @pl.when(x == holder)
    def _():
        for d in range(1, X):
            ca_copy(d).wait_send()

    for k in range(hx):
        @pl.when(x * hx + k != z)
        def _():
            cz_copy(k).wait_send()


def per_device(queries, keys_values, random_blocks, global_blocks, out_proj):
    tokens, width = queries.shape
    bd = tokens // BLK
    nz = lax.axis_size("seq") // X
    head_dim = width // H
    assert nz == H and head_dim == HALF and bd % 2 == 0
    nb = nz * X * bd
    scale2 = 1.4426950408889634 * head_dim ** -0.5
    dma = pltpu.SemaphoreType.DMA
    vm = pl.BlockSpec(memory_space=pltpu.VMEM)
    half_tok = tokens // 2
    hbm = pl.BlockSpec(memory_space=pltpu.HBM)
    nk = lax.axis_size("batch")
    w_rows = out_proj.shape[0]
    return pl.pallas_call(
        functools.partial(kernel, nz, bd, scale2),
        out_shape=jax.ShapeDtypeStruct((tokens, width), BF16),
        in_specs=[pl.BlockSpec(memory_space=pltpu.SMEM), vm, hbm, hbm, hbm],
        out_specs=vm,
        scratch_shapes=[
            pltpu.VMEM((bd, BLK, width), BF16),
            pltpu.VMEM((2, tokens, width), BF16),
            pltpu.VMEM((w_rows, width), BF16),
            pltpu.VMEM((nz, 1, LANES), jnp.int32),
            pltpu.VMEM((tokens, width), F32),
            pltpu.VMEM((nk, X, nz, w_rows, width // nk), BF16),
            pltpu.VMEM((nz, bd // 2, BLK, LANES), BF16),
            pltpu.VMEM((nz, bd, BLK, LANES), BF16),
            pltpu.VMEM((nb + 2, BLK, LANES), BF16),
            pltpu.VMEM((nz, bd // 2, BLK, LANES), BF16),
            pltpu.VMEM((nz, 1, LANES), jnp.int32),
            pltpu.SMEM((nz, 1, LANES), jnp.int32),
            pltpu.VMEM((nz, BLK, LANES), BF16),
            pltpu.VMEM((X, nz // X, BLK, LANES), BF16),
            pltpu.VMEM((nz // X, BLK, LANES), BF16),
            pltpu.VMEM((nz, BLK, LANES), BF16),
            pltpu.VMEM((BLK, LANES), BF16),
            pltpu.VMEM((X, G * BLK, LANES), F32),
            pltpu.VMEM((G * BLK, LANES), F32),
            pltpu.VMEM((G * BLK, LANES), BF16),
            pltpu.VMEM((nz, half_tok, LANES), BF16),
            pltpu.VMEM((nz, half_tok, LANES), BF16),
            pltpu.VMEM((2, G * BLK, LANES), F32),
        ]
        + [dma((nz,))] * 20
        + [dma((X,))] * 7
        + [dma((nk,))] * 2
        + [dma((3,)), dma, dma],
        compiler_params=pltpu.CompilerParams(
            collective_id=0, has_side_effects=True, vmem_limit_bytes=62 * 1024 * 1024
        ),
    )(global_blocks, random_blocks, queries.reshape(bd, BLK, width), keys_values, out_proj)


def solution(mesh):
    placed = (
        P(("batch", "seq"), None),
        P(None, ("batch", "seq"), None),
        P(("batch", "seq"), None, None),
        P("batch"),
        P("seq", None),
    )
    return jax.shard_map(
        per_device, mesh=mesh, in_specs=placed, out_specs=P(("batch", "seq"), None), check_vma=False
    )
```
